128 devices in a mesh: tm: 16 (over x, z), batch: 8 (over y, core).
Axes of the slice: x: 4, y: 4, z: 4, core: 2. Of those that a mesh axis runs over, the one named last changes fastest.
Arguments:
- state: float32 [16, 8, 256, 1152], P('tm', 'batch'), may hold values from -6 to 6
- noise_draws: bfloat16 [2, 16, 8, 256, 1152], P(None, 'tm', 'batch'), may hold values from -6 to 6
- class_vec: float32 [8, 1152], P('batch'), may hold values from -6 to 6
- window_start: int32 [8], P('batch'), may hold values from 0 to 977
- advance: int32 [8], P('batch'), may hold values from 1 to 7
- step_dt: float32 [1000], replicated, may hold values from 0.05 to 0.2
- step_sigma: float32 [1000], replicated, may hold values from 0.05 to 0.2
- w_ada: bfloat16 [1152, 3456], replicated, may hold values from -0.1875 to 0.1875
- w_up: bfloat16 [4608, 1152], P(('tm', 'batch')), may hold values from -0.1875 to 0.1875
- w_down: bfloat16 [4608, 1152], P(('tm', 'batch')), may hold values from -0.09375 to 0.09375
Outputs:
- window_out: float32 [16, 8, 256, 1152], P('tm', 'batch')
The draws below stay inside these ranges and needn't reach their ends.
All inputs are finite; a program needn't handle non-finite values.
Results may differ from the reference program's by a relative error of at most 0.0037.
Values may be sent and summed in bfloat16 or wider, within the bound.
No kernel may reach another device: no remote copies, remote signals or barrier semaphores. Data moves between devices by JAX's collectives and lax.ppermute only.
A program may use at most 128 MiB of HBM per device.

```python
import math
import jax
import jax.numpy as jnp
from jax import lax

D = 1152
LAT = 256
FF = 4608
TRAJ = 1000
SWEEPS = 2
ADV_MAX = 7
WINDOW = 16
IMAGES = 8


def plant(values, rng, low, largest):
    longest = values.shape.index(max(values.shape))
    spots = []
    for shift in (0, 1):
        where = [jax.random.randint(jax.random.fold_in(rng, axis), (), 0, length) for axis, length in enumerate(values.shape)]
        where[longest] = (where[longest] + shift) % values.shape[longest]
        spots.append(tuple(where))
    return values.at[spots[0]].set(low).at[spots[1]].set(largest)


def steps_of(own_key, dims, shards, least, top_value):
    def one(position, shards_of):
        steps = jax.random.uniform(jax.random.fold_in(jax.random.fold_in(own_key, 6), position), (shards_of,), jnp.float32, least / len(shards), top_value / len(shards))
        return jnp.repeat(jnp.exp(steps), dims[position] // shards_of).reshape((-1,) + (1,) * (len(dims) - position - 1))

    loudness = one(*shards[0])
    for cut in shards[1:]:
        loudness = loudness * one(*cut)
    return loudness


def noise(rng, shape, deviation, limit, cuts=(), kind=jnp.bfloat16):
    factor_of = steps_of(rng, shape, cuts, -0.22, 0.18) if cuts else 1.0
    entries = jax.random.normal(rng, shape, jnp.float32) * deviation * factor_of
    return jnp.minimum(jnp.maximum(entries, -limit), limit).astype(kind)


def setup_inputs(seed: int = 0) -> dict:
    keys = jax.random.split(jax.random.key(seed), 11)
    state = noise(keys[0], (WINDOW, IMAGES, LAT, D), 1.0, 6.0, ((0, 16), (1, 8)), jnp.float32)
    noise_draws = noise(keys[1], (SWEEPS, WINDOW, IMAGES, LAT, D), 1.0, 6.0, ((1, 16), (2, 8)))
    class_vec = noise(keys[2], (IMAGES, D), 1.0, 6.0, ((0, 8),), jnp.float32)
    window_start = plant(jax.random.randint(keys[3], (IMAGES,), 0, TRAJ - WINDOW - ADV_MAX + 1), jax.random.fold_in(keys[3], 1), 0, TRAJ - WINDOW - ADV_MAX).astype(jnp.int32)
    advance = plant(jax.random.randint(keys[4], (IMAGES,), 1, ADV_MAX + 1), jax.random.fold_in(keys[4], 1), 1, ADV_MAX).astype(jnp.int32)
    step_dt = jnp.clip(jnp.exp(jax.random.uniform(keys[5], (TRAJ,), jnp.float32, math.log(0.05), math.log(0.2))), 0.05, 0.2)
    step_sigma = jnp.clip(jnp.exp(jax.random.uniform(keys[6], (TRAJ,), jnp.float32, math.log(0.05), math.log(0.2))), 0.05, 0.2)
    w_ada = noise(keys[7], (D, 3 * D), D ** -0.5, 0.1875)
    w_up = noise(keys[8], (FF, D), D ** -0.5, 0.1875, ((0, 128),))
    w_down = noise(keys[9], (FF, D), FF ** -0.5, 0.09375, ((0, 128),))
    return dict(state=state, noise_draws=noise_draws, class_vec=class_vec, window_start=window_start, advance=advance, step_dt=step_dt, step_sigma=step_sigma, w_ada=w_ada, w_up=w_up, w_down=w_down)


EPSILON = 1e-06

def time_embed(steps_now, half_width):
    frequency = jnp.exp(-math.log(10000.0) * jnp.arange(half_width, dtype=jnp.float32) / half_width)
    angles = steps_now.astype(jnp.float32)[:, None] * frequency[None, :]
    return jnp.concatenate([jnp.cos(angles), jnp.sin(angles)], axis=1)

def dense_pair(hidden_rows, up_rows, down_rows):
    before = lax.dot_general(hidden_rows, up_rows, (((1,), (1,)), ((), ())), preferred_element_type=jnp.float32)
    activated = jax.nn.gelu(before, approximate=True).astype(jnp.bfloat16)
    return jnp.dot(activated, down_rows, preferred_element_type=jnp.float32)

def increment(current, noise_now, steps_now, class_vec, step_dt, step_sigma, w_ada, w_up, w_down):
    images, tokens, channels = current.shape
    step_table = lax.iota(jnp.int32, step_dt.shape[0])
    onehot = (steps_now[:, None] == step_table[None, :]).astype(jnp.float32)
    step_size = lax.optimization_barrier(jnp.sum(onehot * step_dt[None, :], axis=1))
    spread = lax.optimization_barrier(jnp.sum(onehot * step_sigma[None, :], axis=1))
    condition = jax.nn.silu(time_embed(steps_now, channels // 2) + class_vec).astype(jnp.bfloat16)
    modulation = jnp.dot(condition, w_ada, preferred_element_type=jnp.float32)
    shift_by = modulation[:, :channels]
    scale_by = modulation[:, channels:2 * channels]
    gate_by = modulation[:, 2 * channels:]
    mean_val = lax.optimization_barrier(jnp.mean(current, axis=2, keepdims=True))
    centred = current - mean_val
    var_val = lax.optimization_barrier(jnp.mean(centred * centred, axis=2, keepdims=True))
    normed = centred * lax.rsqrt(var_val + EPSILON)
    hidden_in = (normed * (1.0 + scale_by[:, None, :]) + shift_by[:, None, :]).astype(jnp.bfloat16)
    mlp_out = dense_pair(hidden_in.reshape(images * tokens, channels), w_up, w_down).reshape(images, tokens, channels)
    drift = gate_by[:, None, :] * mlp_out - current
    return step_size[:, None, None] * drift + spread[:, None, None] * noise_now.astype(jnp.float32)

def pick_rows(column, source_index):
    return column[source_index]

def reference(state, noise_draws, class_vec, window_start, advance, step_dt, step_sigma, w_ada, w_up, w_down):
    window_size = state.shape[0]

    def sweep(states, noise_now, starts):

        def one_step(items):
            current, noise_step, offset = items
            return increment(current, noise_step, starts + offset, class_vec, step_dt, step_sigma, w_ada, w_up, w_down)
        increments = lax.map(one_step, (states, noise_now, jnp.arange(window_size, dtype=jnp.int32)))
        totals = jnp.cumsum(increments, axis=0)
        exclusive = jnp.concatenate([jnp.zeros_like(increments[:1]), totals[:-1]], axis=0)
        updated = states[0][None] + exclusive
        end_rows = states[0] + totals[-1]
        return (updated, end_rows)
    updated, end_rows = sweep(state, noise_draws[0], window_start)
    extended = jnp.concatenate([updated, end_rows[None]], axis=0)
    source_index = jnp.minimum(jnp.arange(window_size, dtype=jnp.int32)[:, None] + advance[None, :], window_size)
    slid = jax.vmap(pick_rows, in_axes=(1, 1), out_axes=1)(extended, source_index)
    final_rows, leftover = sweep(slid, noise_draws[1], window_start + advance)
    return final_rows
```

```python
import functools
import math

import jax
import jax.numpy as jnp
from jax import lax
from jax.experimental import pallas as pl
from jax.experimental.pallas import tpu as pltpu
from jax.sharding import PartitionSpec as P

EPSILON = 1e-06
ALL = ("tm", "batch")
SIDE = 4
CORES = 2
THIRDS = 3
SLIDE = 7
f32, bf16 = jnp.float32, jnp.bfloat16


def device_pairs(move):
    pairs = []
    for x in range(SIDE):
        for z in range(SIDE):
            for y in range(SIDE):
                for core in range(CORES):
                    here, there = (x, z, y, core), move((x, z, y, core))
                    flat = [((p[0] * SIDE + p[1]) * SIDE + p[2]) * CORES + p[3] for p in (here, there)]
                    pairs.append(tuple(flat))
    return pairs


def neighbour(axis, first):
    def move(place):
        place = list(place)
        odd = (place[3] == 0) == first
        place[axis] = place[axis] ^ 1 if odd else SIDE - 1 - place[axis]
        return tuple(place)

    return device_pairs(move)


def send(rows, axis, first):
    return lax.ppermute(rows, ALL, neighbour(axis, first))


def swap_cores(rows):
    return lax.ppermute(rows, ALL, device_pairs(lambda p: (p[0], p[1], p[2], 1 - p[3])))


def grow(rows, axis, core):
    near = send(rows, axis, True)
    both = send(jnp.concatenate([rows, near]), axis, False)
    count = rows.shape[0]
    second, far = both[:count], both[count:]
    low = jnp.where(core == 0, near, second)
    high = jnp.where(core == 0, second, near)
    return jnp.concatenate([rows, low, high, far])


def gelu(before):
    inner = math.sqrt(2.0 / math.pi) * (before + 0.044715 * (before * before * before))
    return 0.5 * before * (1.0 + jnp.tanh(inner))


def copies(side, pairs, up_buf, down_buf, sems, slot):
    made = []
    size = pairs[0][0].shape[0]
    for part, pair in enumerate(pairs):
        place = pl.ds(part * size, size)
        made.append(pltpu.make_async_copy(pair[side], up_buf.at[slot, place], sems.at[slot, 0, part]))
        made.append(
            pltpu.make_async_copy(pair[1 - side], down_buf.at[slot, place], sems.at[slot, 1, part])
        )
    return made


def start_set(core_ref, *where):
    for side in (0, 1):

        @pl.when(core_ref[0] == side)
        def _():
            for copy in copies(side, *where):
                copy.start()


def wait_set(*where):
    for copy in copies(0, *where):
        copy.wait()


def mlp_sets(core_ref, sets, hidden_ref, acc_ref, fresh, up_buf, down_buf, sems):
    for index, pairs in enumerate(sets):
        slot = index % 2
        if index + 1 < len(sets):
            start_set(core_ref, sets[index + 1], up_buf, down_buf, sems, 1 - slot)
        wait_set(pairs, up_buf, down_buf, sems, slot)
        before = lax.dot_general(
            hidden_ref[...], up_buf[slot], (((1,), (1,)), ((), ())), preferred_element_type=f32
        )
        part = jnp.dot(gelu(before).astype(bf16), down_buf[slot], preferred_element_type=f32)
        if fresh and index == 0:
            acc_ref[...] = part
        else:
            acc_ref[...] += part


def as_sets(refs):
    pairs = [(refs[i], refs[i + 1]) for i in range(0, len(refs), 2)]
    return [pairs[i : i + THIRDS] for i in range(0, len(pairs), THIRDS)]


def weight_scratch(units, width, slots):
    return [
        pltpu.VMEM((slots, units, width), bf16),
        pltpu.VMEM((slots, units, width), bf16),
        pltpu.SemaphoreType.DMA((slots, 2, THIRDS)),
    ]


def flat_sets(sets):
    return [array for pairs in sets for pair in pairs for array in pair]


SMEM = pl.BlockSpec(memory_space=pltpu.SMEM)
VMEM = pl.BlockSpec(memory_space=pltpu.VMEM)
ANY = pl.BlockSpec(memory_space=pl.ANY)
PARAMS = pltpu.CompilerParams(vmem_limit_bytes=36 * 2**20)


def piece_kernel(count, fresh, core_ref, hidden_ref, *refs):
    acc_in = None if fresh else refs[0]
    refs = refs if fresh else refs[1:]
    sets = as_sets(refs[:count])
    acc_ref, up_buf, down_buf, sems = refs[count:]
    start_set(core_ref, sets[0], up_buf, down_buf, sems, 0)
    if not fresh:
        acc_ref[...] = acc_in[...]
    mlp_sets(core_ref, sets, hidden_ref, acc_ref, fresh, up_buf, down_buf, sems)


def mlp_piece(core, hidden, acc, sets):
    weights = flat_sets(sets)
    units = THIRDS * weights[0].shape[0]
    fresh = acc is None
    given = [] if fresh else [acc]
    return pl.pallas_call(
        functools.partial(piece_kernel, len(weights), fresh),
        out_shape=jax.ShapeDtypeStruct(hidden.shape, f32),
        in_specs=[SMEM, VMEM] + [VMEM] * len(given) + [ANY] * len(weights),
        out_specs=VMEM,
        scratch_shapes=weight_scratch(units, hidden.shape[1], min(2, len(sets))),
        compiler_params=PARAMS,
        name="mlp_piece",
    )(core, hidden, *given, *weights)


def finish_kernel(
    count, core_ref, first_ref, step_ref, hidden_ref, acc_in, state_ref, noise_ref, later_ref, gate_ref, *refs
):
    sets = as_sets(refs[:count])
    out_ref, acc_ref, up_buf, down_buf, sems = refs[count:]
    start_set(core_ref, sets[0], up_buf, down_buf, sems, 0)
    acc_ref[...] = acc_in[...]
    mlp_sets(core_ref, sets, hidden_ref, acc_ref, False, up_buf, down_buf, sems)
    peers, rows, _ = out_ref.shape
    rows = rows // 3
    gate = gate_ref[...]

    def one(peer, carry):
        place = pl.ds(pl.multiple_of(peer * rows, rows), rows)
        state = state_ref[place, :]
        drift = gate * acc_ref[place, :] - state
        inc = step_ref[0] * drift + step_ref[1] * noise_ref[place, :].astype(f32)
        inc = inc + first_ref[0] * state
        high = inc.astype(bf16)
        out_ref[peer, 0:rows, :] = high
        out_ref[peer, rows : 2 * rows, :] = (inc - high.astype(f32)).astype(bf16)
        out_ref[peer, 2 * rows : 3 * rows, :] = later_ref[place, :]
        return carry

    lax.fori_loop(0, peers, one, 0)


def finish_first(core, is_first, step, hidden, acc, state, noise, later, gate, sets, peers):
    weights = flat_sets(sets)
    units = THIRDS * weights[0].shape[0]
    tokens, width = hidden.shape
    return pl.pallas_call(
        functools.partial(finish_kernel, len(weights)),
        out_shape=jax.ShapeDtypeStruct((peers, 3 * (tokens // peers), width), bf16),
        in_specs=[SMEM] * 3 + [VMEM] * 6 + [ANY] * len(weights),
        out_specs=VMEM,
        scratch_shapes=[pltpu.VMEM((tokens, width), f32)] + weight_scratch(units, width, 1),
        compiler_params=PARAMS,
        name="finish_first",
    )(core, is_first, step, hidden, acc, state, noise, later, gate, *weights)


def second_kernel(count, core_ref, advance_ref, dt_ref, sigma_ref, got_ref, shift_ref, scale_ref, gate_ref, *refs):
    sets = as_sets(refs[:count])
    out_ref, prefix_ref, hidden_ref, acc_ref, up_buf, down_buf, sems = refs[count:]
    start_set(core_ref, sets[0], up_buf, down_buf, sems, 0)
    window, rows, width = out_ref.shape
    advance = advance_ref[0]

    total = jnp.zeros((rows, width), f32)
    for place in range(window):
        inc = got_ref[place, 0:rows, :].astype(f32) + got_ref[place, rows : 2 * rows, :].astype(f32)
        total = total + inc
        prefix_ref[place + 1] = total
    for place in range(window + 1, window + SLIDE):
        prefix_ref[place] = total

    def modulate(place, carry):
        state = prefix_ref[place + advance]
        mean = jnp.mean(state, axis=1, keepdims=True)
        centred = state - mean
        var = jnp.mean(centred * centred, axis=1, keepdims=True)
        normed = centred * lax.rsqrt(var + EPSILON)
        hidden = normed * (1.0 + scale_ref[pl.ds(place, 1), :]) + shift_ref[pl.ds(place, 1), :]
        hidden_ref[pl.ds(pl.multiple_of(place * rows, rows), rows), :] = hidden.astype(bf16)
        return carry

    lax.fori_loop(0, window, modulate, 0)
    mlp_sets(core_ref, sets, hidden_ref, acc_ref, True, up_buf, down_buf, sems)

    def advance_one(place, updated):
        out_ref[place] = updated.astype(bf16)
        state = prefix_ref[place + advance]
        mlp_out = acc_ref[pl.ds(pl.multiple_of(place * rows, rows), rows), :]
        drift = gate_ref[pl.ds(place, 1), :] * mlp_out - state
        noise = got_ref[place, 2 * rows : 3 * rows, :].astype(f32)
        return updated + (dt_ref[place] * drift + sigma_ref[place] * noise)

    lax.fori_loop(0, window, advance_one, prefix_ref[advance])


def second_sweep(core, advance, dt, sigma, got, shift, scale, gate, sets):
    weights = flat_sets(sets)
    units = THIRDS * weights[0].shape[0]
    window, rows, width = got.shape
    rows = rows // 3
    return pl.pallas_call(
        functools.partial(second_kernel, len(weights)),
        out_shape=jax.ShapeDtypeStruct((window, rows, width), bf16),
        in_specs=[SMEM] * 4 + [VMEM] * 4 + [ANY] * len(weights),
        out_specs=VMEM,
        scratch_shapes=[
            pltpu.VMEM((window + SLIDE + 1, rows, width), f32),
            pltpu.VMEM((window * rows, width), bf16),
            pltpu.VMEM((window * rows, width), f32),
        ]
        + weight_scratch(units, width, 2),
        compiler_params=PARAMS,
        name="second_sweep",
    )(core, advance, dt, sigma, got, shift, scale, gate, *weights)


def time_embed(steps_now, half_width):
    frequency = jnp.exp(-math.log(10000.0) * jnp.arange(half_width, dtype=f32) / half_width)
    angles = steps_now.astype(f32)[:, None] * frequency[None, :]
    return jnp.concatenate([jnp.cos(angles), jnp.sin(angles)], axis=1)


def per_device(
    state, noise_draws, class_vec, window_start, advance, step_dt, step_sigma, w_ada, w_up, w_down
):
    window = lax.axis_size("tm")
    position = lax.axis_index("tm")
    core = lax.axis_index("batch") % CORES
    core_arg = core.astype(jnp.int32)[None]
    state, noise_now, noise_later = state[0, 0], noise_draws[0, 0, 0], noise_draws[1, 0, 0]
    tokens, width = state.shape

    other = swap_cores(jnp.where(core == 0, w_down, w_up))
    rows = jnp.where(
        core == 0, jnp.concatenate([w_up, other]), jnp.concatenate([other, w_down])
    )
    third = rows.shape[0] // THIRDS
    parts = [rows[i * third : (i + 1) * third] for i in range(THIRDS)]
    orders = [(0, 1, 2), (1, 2, 0), (2, 0, 1)]
    for phase in range(2):
        parts = [grow(part, order[phase], core) for part, order in zip(parts, orders)]

    last = [order[2] for order in orders]
    first = [send(part, axis, True) for part, axis in zip(parts, last)]
    second = [send(part, axis, False) for part, axis in zip(parts, last)]
    own_swapped = [swap_cores(part) for part in parts]
    far = [send(part, axis, False) for part, axis in zip(first, last)]
    first_swapped = [swap_cores(part) for part in first]
    second_swapped = [swap_cores(part) for part in second]
    far_swapped = [swap_cores(part) for part in far]
    set_own = list(zip(parts, own_swapped))
    set_low = list(zip(first, second_swapped))
    set_high = list(zip(second, first_swapped))
    set_far = list(zip(far, far_swapped))

    begin, ahead = window_start[0], advance[0]
    steps = jnp.concatenate(
        [
            begin + ahead + jnp.arange(window, dtype=jnp.int32),
            jnp.full((8,), begin + position, jnp.int32),
        ]
    )
    condition = jax.nn.silu(time_embed(steps, width // 2) + class_vec).astype(bf16)
    modulation = jnp.dot(condition, w_ada, preferred_element_type=f32)
    shift_by, scale_by, gate_by = (modulation[:, i * width : (i + 1) * width] for i in range(3))
    own = slice(window, window + 1)

    mean = jnp.mean(state, axis=1, keepdims=True)
    centred = state - mean
    var = jnp.mean(centred * centred, axis=1, keepdims=True)
    normed = centred * lax.rsqrt(var + EPSILON)
    hidden = (normed * (1.0 + scale_by[own]) + shift_by[own]).astype(bf16)

    step_now = jnp.stack(
        [
            lax.dynamic_index_in_dim(step_dt, begin + position, 0, False),
            lax.dynamic_index_in_dim(step_sigma, begin + position, 0, False),
        ]
    )
    dt_later = lax.dynamic_slice(step_dt, (begin + ahead,), (window,))
    sigma_later = lax.dynamic_slice(step_sigma, (begin + ahead,), (window,))
    is_first = (position == 0).astype(f32)[None]

    acc = mlp_piece(core_arg, hidden, None, [set_own])
    acc = mlp_piece(core_arg, hidden, acc, [set_low, set_high])
    sent = finish_first(
        core_arg, is_first, step_now, hidden, acc, state, noise_now, noise_later, gate_by[own], [set_far], window
    )
    got = lax.all_to_all(sent, "tm", 0, 0, tiled=True)
    updated = second_sweep(
        core_arg,
        advance,
        dt_later,
        sigma_later,
        got,
        shift_by[:window],
        scale_by[:window],
        gate_by[:window],
        [set_own, set_low, set_high, set_far],
    )
    final = lax.all_to_all(updated, "tm", 0, 0, tiled=True)
    return final.reshape(1, 1, tokens, width).astype(f32)


def solution(mesh):
    in_specs = (
        P("tm", "batch", None, None),
        P(None, "tm", "batch", None, None),
        P("batch", None),
        P("batch"),
        P("batch"),
        P(),
        P(),
        P(),
        P(("tm", "batch"), None),
        P(("tm", "batch"), None),
    )
    out_specs = P("tm", "batch", None, None)
    return jax.shard_map(
        per_device, mesh=mesh, in_specs=in_specs, out_specs=out_specs, check_vma=False
    )
```

```python
import functools
import math

import jax
import jax.numpy as jnp
from jax import lax
from jax.experimental import pallas as pl
from jax.experimental.pallas import tpu as pltpu
from jax.sharding import PartitionSpec as P

EPSILON = 1e-06
ALL = ("tm", "batch")
SIDE = 4
CORES = 2
THIRDS = 3
SLIDE = 7
ROWS = 16
OWN_ROW = slice(16, 17)
f32, bf16 = jnp.float32, jnp.bfloat16


def device_pairs(move):
    pairs = []
    for x in range(SIDE):
        for z in range(SIDE):
            for y in range(SIDE):
                for core in range(CORES):
                    here, there = (x, z, y, core), move((x, z, y, core))
                    flat = [((p[0] * SIDE + p[1]) * SIDE + p[2]) * CORES + p[3] for p in (here, there)]
                    pairs.append(tuple(flat))
    return pairs


def neighbour(axis, first):
    def move(place):
        place = list(place)
        odd = (place[3] == 0) == first
        place[axis] = place[axis] ^ 1 if odd else SIDE - 1 - place[axis]
        return tuple(place)

    return device_pairs(move)


def send(rows, axis, first):
    return lax.ppermute(rows, ALL, neighbour(axis, first))


def swap_cores(rows):
    return lax.ppermute(rows, ALL, device_pairs(lambda p: (p[0], p[1], p[2], 1 - p[3])))


def grow(rows, axis, core):
    near = send(rows, axis, True)
    both = send(jnp.concatenate([rows, near]), axis, False)
    count = rows.shape[0]
    second, far = both[:count], both[count:]
    low = jnp.where(core == 0, near, second)
    high = jnp.where(core == 0, second, near)
    return jnp.concatenate([rows, low, high, far])


def gelu(before):
    inner = math.sqrt(2.0 / math.pi) * (before + 0.044715 * (before * before * before))
    return 0.5 * before * (1.0 + jnp.tanh(inner))


def copies(side, pairs, up_buf, down_buf, sems, slot):
    made = []
    size = pairs[0][0].shape[0]
    for part, pair in enumerate(pairs):
        place = pl.ds(part * size, size)
        made.append(pltpu.make_async_copy(pair[side], up_buf.at[slot, place], sems.at[slot, 0, part]))
        made.append(
            pltpu.make_async_copy(pair[1 - side], down_buf.at[slot, place], sems.at[slot, 1, part])
        )
    return made


def start_set(core_ref, *where):
    for side in (0, 1):

        @pl.when(core_ref[0] == side)
        def _():
            for copy in copies(side, *where):
                copy.start()


def wait_set(*where):
    for copy in copies(0, *where):
        copy.wait()


def mlp_part(hidden, up_rows, down_rows):
    before = lax.dot_general(hidden, up_rows, (((1,), (1,)), ((), ())), preferred_element_type=f32)
    return jnp.dot(gelu(before).astype(bf16), down_rows, preferred_element_type=f32)


def mlp_sets(core_ref, sets, kept_refs, hidden_ref, acc_ref, given, up_buf, down_buf, sems, kept_sems):
    kept = []
    for index, pairs in enumerate(sets):
        slot = index % 2
        if index + 1 < len(sets):
            start_set(core_ref, sets[index + 1], up_buf, down_buf, sems, 1 - slot)
        wait_set(pairs, up_buf, down_buf, sems, slot)
        for kind, buf in enumerate((up_buf, down_buf)):
            place = 2 * index + kind
            kept.append(pltpu.make_async_copy(buf.at[slot], kept_refs[place], kept_sems.at[place]))
            kept[-1].start()
        part = mlp_part(hidden_ref[...], up_buf[slot], down_buf[slot])
        if index > 0:
            acc_ref[...] += part
        elif given is None:
            acc_ref[...] = part
        else:
            acc_ref[...] = given[...] + part
    for copy in kept:
        copy.wait()


def as_sets(refs):
    pairs = [(refs[i], refs[i + 1]) for i in range(0, len(refs), 2)]
    return [pairs[i : i + THIRDS] for i in range(0, len(pairs), THIRDS)]


def weight_scratch(units, width, slots):
    return [
        pltpu.VMEM((slots, units, width), bf16),
        pltpu.VMEM((slots, units, width), bf16),
        pltpu.SemaphoreType.DMA((slots, 2, THIRDS)),
        pltpu.SemaphoreType.DMA((2 * slots,)),
    ]


def kept_shapes(units, width, slots):
    return [jax.ShapeDtypeStruct((units, width), bf16)] * (2 * slots)


def flat_sets(sets):
    return [array for pairs in sets for pair in pairs for array in pair]


SMEM = pl.BlockSpec(memory_space=pltpu.SMEM)
VMEM = pl.BlockSpec(memory_space=pltpu.VMEM)
ANY = pl.BlockSpec(memory_space=pl.ANY)
HBM = pl.BlockSpec(memory_space=pltpu.HBM)
MIB = 2**20


def room(mebibytes):
    return pltpu.CompilerParams(vmem_limit_bytes=mebibytes * MIB)


def modulated(state, shift_row, scale_row):
    mean = jnp.mean(state, axis=1, keepdims=True)
    centred = state - mean
    var = jnp.mean(centred * centred, axis=1, keepdims=True)
    normed = centred * lax.rsqrt(var + EPSILON)
    return (normed * (1.0 + scale_row) + shift_row).astype(bf16)


def block_of(place, rows):
    return pl.ds(pl.multiple_of(place * rows, rows), rows)


def own_kernel(count, core_ref, state_ref, mod_ref, *refs):
    sets = as_sets(refs[:count])
    hidden_ref, acc_ref, *weights = refs[count:]
    kept, weights = weights[:2], weights[2:]
    start_set(core_ref, sets[0], *weights[:3], 0)
    tokens, width = state_ref.shape

    def one(place, carry):
        rows = block_of(place, ROWS)
        hidden_ref[rows, :] = modulated(
            state_ref[rows, :], mod_ref[OWN_ROW, 0:width], mod_ref[OWN_ROW, width : 2 * width]
        )
        return carry

    lax.fori_loop(0, tokens // ROWS, one, 0)
    mlp_sets(core_ref, sets, kept, hidden_ref, acc_ref, None, *weights)


def own_piece(core, state, mod, sets):
    weights = flat_sets(sets)
    units = THIRDS * weights[0].shape[0]
    tokens, width = state.shape
    return pl.pallas_call(
        functools.partial(own_kernel, len(weights)),
        out_shape=[jax.ShapeDtypeStruct((tokens, width), bf16), jax.ShapeDtypeStruct((tokens, width), f32)]
        + kept_shapes(units, width, 1),
        in_specs=[SMEM, VMEM, VMEM] + [ANY] * len(weights),
        out_specs=[VMEM, VMEM, HBM, HBM],
        scratch_shapes=weight_scratch(units, width, 1),
        compiler_params=room(56),
        name="own_piece",
    )(core, state, mod, *weights)


def next_kernel(count, core_ref, hidden_ref, acc_in, *refs):
    sets = as_sets(refs[:count])
    acc_ref, *weights = refs[count:]
    kept, weights = weights[:4], weights[4:]
    start_set(core_ref, sets[0], *weights[:3], 0)
    mlp_sets(core_ref, sets, kept, hidden_ref, acc_ref, acc_in, *weights)


def next_piece(core, hidden, acc, sets):
    weights = flat_sets(sets)
    units = THIRDS * weights[0].shape[0]
    tokens, width = hidden.shape
    return pl.pallas_call(
        functools.partial(next_kernel, len(weights)),
        out_shape=[jax.ShapeDtypeStruct((tokens, width), f32)] + kept_shapes(units, width, 2),
        in_specs=[SMEM, VMEM, VMEM] + [ANY] * len(weights),
        out_specs=[VMEM] + [HBM] * 4,
        scratch_shapes=weight_scratch(units, width, 2),
        compiler_params=room(56),
        name="next_piece",
    )(core, hidden, acc, *weights)


def far_kernel(
    count, core_ref, first_ref, begin_ref, dt_ref, sigma_ref, hidden_ref, acc_in, state_ref, noise_ref, mod_ref, *refs
):
    sets = as_sets(refs[:count])
    out_ref, up_kept, down_kept, acc_ref, state_buf, noise_buf, own_sems, *weights = refs[count:]
    start_set(core_ref, sets[0], *weights[:3], 0)
    own = [
        pltpu.make_async_copy(state_ref, state_buf, own_sems.at[0]),
        pltpu.make_async_copy(noise_ref, noise_buf, own_sems.at[1]),
    ]
    for copy in own:
        copy.start()
    mlp_sets(core_ref, sets, [up_kept, down_kept], hidden_ref, acc_ref, acc_in, *weights)
    for copy in own:
        copy.wait()
    peers, rows, width = out_ref.shape
    rows = rows // 2
    step = begin_ref[0]

    def one(peer, carry):
        place = block_of(peer, rows)
        state = state_buf[place, :]
        drift = mod_ref[OWN_ROW, 2 * width : 3 * width] * acc_ref[place, :] - state
        inc = dt_ref[step] * drift + sigma_ref[step] * noise_buf[0, place, :].astype(f32)
        out_ref[peer, 0:rows, :] = (inc + first_ref[0] * state).astype(bf16)
        out_ref[peer, rows : 2 * rows, :] = noise_buf[1, place, :]
        return carry

    lax.fori_loop(0, peers, one, 0)


def far_piece(core, is_first, step, dt, sigma, hidden, acc, state, noise, mod, sets, peers):
    weights = flat_sets(sets)
    units = THIRDS * weights[0].shape[0]
    tokens, width = hidden.shape
    return pl.pallas_call(
        functools.partial(far_kernel, len(weights)),
        out_shape=[jax.ShapeDtypeStruct((peers, 2 * (tokens // peers), width), bf16)]
        + kept_shapes(units, width, 1),
        in_specs=[SMEM] * 5 + [VMEM] * 2 + [ANY] * 2 + [VMEM] + [ANY] * len(weights),
        out_specs=[VMEM, HBM, HBM],
        scratch_shapes=[
            pltpu.VMEM((tokens, width), f32),
            pltpu.VMEM(state.shape, f32),
            pltpu.VMEM(noise.shape, bf16),
            pltpu.SemaphoreType.DMA((2,)),
        ]
        + weight_scratch(units, width, 1),
        compiler_params=room(56),
        name="far_piece",
    )(core, is_first, step, dt, sigma, hidden, acc, state, noise, mod, *weights)


def second_kernel(count, begin_ref, advance_ref, dt_ref, sigma_ref, got_ref, mod_ref, *refs):
    sets = [(refs[i], refs[i + 1]) for i in range(0, count, 2)]
    out_ref, prefix_ref, hidden_ref, acc_ref, up_buf, down_buf, sems = refs[count:]

    def copies(index):
        slot = index % 2
        return [
            pltpu.make_async_copy(sets[index][kind], buf.at[slot], sems.at[slot, kind, 0])
            for kind, buf in enumerate((up_buf, down_buf))
        ]

    for copy in copies(0):
        copy.start()
    window, rows, width = out_ref.shape
    advance = advance_ref[0]
    begin = begin_ref[0] + advance

    total = got_ref[0, 0:rows, :].astype(f32)
    for place in range(1, window + SLIDE):
        prefix_ref[place] = total
        if place < window:
            total = total + got_ref[place, 0:rows, :].astype(f32)

    def modulate(place, carry):
        row = pl.ds(place, 1)
        hidden_ref[block_of(place, rows), :] = modulated(
            prefix_ref[place + advance], mod_ref[row, 0:width], mod_ref[row, width : 2 * width]
        )
        return carry

    lax.fori_loop(0, window, modulate, 0)
    for index in range(len(sets)):
        if index + 1 < len(sets):
            for copy in copies(index + 1):
                copy.start()
        for copy in copies(index):
            copy.wait()
        part = mlp_part(hidden_ref[...], up_buf[index % 2], down_buf[index % 2])
        acc_ref[...] = part if index == 0 else acc_ref[...] + part

    def update(place, updated):
        out_ref[place] = updated.astype(bf16)
        gate = mod_ref[pl.ds(place, 1), 2 * width : 3 * width]
        drift = gate * acc_ref[block_of(place, rows), :] - prefix_ref[place + advance]
        noise = got_ref[place, rows : 2 * rows, :].astype(f32)
        return updated + (dt_ref[begin + place] * drift + sigma_ref[begin + place] * noise)

    lax.fori_loop(0, window, update, prefix_ref[advance])


def second_sweep(begin, advance, dt, sigma, got, mod, weights):
    units = weights[0].shape[0]
    window, rows, width = got.shape
    rows = rows // 2
    return pl.pallas_call(
        functools.partial(second_kernel, len(weights)),
        out_shape=jax.ShapeDtypeStruct((window, rows, width), bf16),
        in_specs=[SMEM] * 4 + [VMEM] * 2 + [HBM] * len(weights),
        out_specs=VMEM,
        scratch_shapes=[
            pltpu.VMEM((window + SLIDE, rows, width), f32),
            pltpu.VMEM((window * rows, width), bf16),
            pltpu.VMEM((window * rows, width), f32),
        ]
        + weight_scratch(units, width, 2)[:3],
        compiler_params=room(56),
        name="second_sweep",
    )(begin, advance, dt, sigma, got, mod, *weights)


def time_embed(steps_now, half_width):
    frequency = jnp.exp(-math.log(10000.0) * jnp.arange(half_width, dtype=f32) / half_width)
    angles = steps_now.astype(f32)[:, None] * frequency[None, :]
    return jnp.concatenate([jnp.cos(angles), jnp.sin(angles)], axis=1)


def after(array, *others):
    return lax.optimization_barrier((array, *others))[0]


def per_device(
    state, noise_draws, class_vec, window_start, advance, step_dt, step_sigma, w_ada, w_up, w_down
):
    window = lax.axis_size("tm")
    core = lax.axis_index("batch") % CORES
    core_arg = core.astype(jnp.int32)[None]
    state, noise = state[0, 0], noise_draws[:, 0, 0]
    tokens, width = state.shape

    other = swap_cores(jnp.where(core == 0, w_down, w_up))
    rows = jnp.where(
        core == 0, jnp.concatenate([w_up, other]), jnp.concatenate([other, w_down])
    )
    third = rows.shape[0] // THIRDS
    parts = [rows[i * third : (i + 1) * third] for i in range(THIRDS)]
    orders = [(0, 1, 2), (1, 2, 0), (2, 0, 1)]
    for phase in range(2):
        parts = [grow(part, order[phase], core) for part, order in zip(parts, orders)]

    begin, ahead = window_start[0], advance[0]
    own_step = begin + lax.axis_index("tm")
    steps = begin + ahead + jnp.arange(window, dtype=jnp.int32)
    steps = jnp.concatenate([steps, jnp.full((8,), own_step, jnp.int32)])
    condition = jax.nn.silu(time_embed(steps, width // 2) + class_vec).astype(bf16)
    modulation = jnp.dot(condition, w_ada, preferred_element_type=f32)
    is_first = (lax.axis_index("tm") == 0).astype(f32)[None]

    last = [order[2] for order in orders]
    parts = [after(part, *parts) for part in parts]
    first = [send(part, axis, True) for part, axis in zip(parts, last)]
    ready = [after(part, near, modulation) for part, near in zip(parts, first)]
    second = [send(part, axis, False) for part, axis in zip(ready, last)]
    own_swapped = [swap_cores(after(part, modulation)) for part in parts]
    first_swapped = [swap_cores(after(part, *own_swapped)) for part in first]
    set_own = list(zip(parts, own_swapped))
    hidden, acc, *kept = own_piece(core_arg, state, modulation, [set_own])
    far = [send(after(near, other, acc), axis, False) for near, other, axis in zip(first, second, last)]
    second_swapped = [swap_cores(part) for part in second]
    set_low = list(zip(first, second_swapped))
    set_high = list(zip(second, first_swapped))
    acc, *more = next_piece(core_arg, hidden, acc, [set_low, set_high])
    kept += more

    far_swapped = [swap_cores(after(part, acc)) for part in far]
    set_far = list(zip(far, far_swapped))
    sent, *more = far_piece(
        core_arg, is_first, own_step[None], step_dt, step_sigma, hidden, acc, state, noise, modulation, [set_far], window
    )
    got = lax.all_to_all(sent, "tm", 0, 0, tiled=True)
    updated = second_sweep(
        window_start,
        advance,
        step_dt,
        step_sigma,
        got,
        modulation,
        kept + more,
    )
    final = lax.all_to_all(updated, "tm", 0, 0, tiled=True)
    return final.reshape(1, 1, tokens, width).astype(f32)


def solution(mesh):
    in_specs = (
        P("tm", "batch", None, None),
        P(None, "tm", "batch", None, None),
        P("batch", None),
        P("batch"),
        P("batch"),
        P(),
        P(),
        P(),
        P(("tm", "batch"), None),
        P(("tm", "batch"), None),
    )
    out_specs = P("tm", "batch", None, None)
    return jax.shard_map(
        per_device, mesh=mesh, in_specs=in_specs, out_specs=out_specs, check_vma=False
    )
```

```python
import functools
import math

import jax
import jax.numpy as jnp
from jax import lax
from jax.experimental import pallas as pl
from jax.experimental.pallas import tpu as pltpu
from jax.sharding import PartitionSpec as P

EPSILON = 1e-06
ALL = ("tm", "batch")
SIDE = 4
CORES = 2
THIRDS = 3
SLIDE = 7
ROWS = 16
OWN_ROW = slice(16, 17)
f32, bf16 = jnp.float32, jnp.bfloat16


def device_pairs(move):
    pairs = []
    for x in range(SIDE):
        for z in range(SIDE):
            for y in range(SIDE):
                for core in range(CORES):
                    here, there = (x, z, y, core), move((x, z, y, core))
                    flat = [((p[0] * SIDE + p[1]) * SIDE + p[2]) * CORES + p[3] for p in (here, there)]
                    pairs.append(tuple(flat))
    return pairs


def neighbour(axis, first):
    def move(place):
        place = list(place)
        odd = (place[3] == 0) == first
        place[axis] = place[axis] ^ 1 if odd else SIDE - 1 - place[axis]
        return tuple(place)

    return device_pairs(move)


def send(rows, axis, first):
    return lax.ppermute(rows, ALL, neighbour(axis, first))


def swap_cores(rows):
    return lax.ppermute(rows, ALL, device_pairs(lambda p: (p[0], p[1], p[2], 1 - p[3])))


def grow(rows, axis, core):
    near = send(rows, axis, True)
    both = send(jnp.concatenate([rows, near]), axis, False)
    count = rows.shape[0]
    second, far = both[:count], both[count:]
    low = jnp.where(core == 0, near, second)
    high = jnp.where(core == 0, second, near)
    return jnp.concatenate([rows, low, high, far])


def gelu(before):
    inner = math.sqrt(2.0 / math.pi) * (before + 0.044715 * (before * before * before))
    return 0.5 * before * (1.0 + jnp.tanh(inner))


def copies(side, pairs, up_buf, down_buf, sems, slot):
    made = []
    size = pairs[0][0].shape[0]
    for part, pair in enumerate(pairs):
        place = pl.ds(part * size, size)
        made.append(pltpu.make_async_copy(pair[side], up_buf.at[slot, place], sems.at[slot, 0, part]))
        made.append(
            pltpu.make_async_copy(pair[1 - side], down_buf.at[slot, place], sems.at[slot, 1, part])
        )
    return made


def start_set(core_ref, *where):
    for side in (0, 1):

        @pl.when(core_ref[0] == side)
        def _():
            for copy in copies(side, *where):
                copy.start()


def wait_set(*where):
    for copy in copies(0, *where):
        copy.wait()


def mlp_part(hidden, up_rows, down_rows):
    before = lax.dot_general(hidden, up_rows, (((1,), (1,)), ((), ())), preferred_element_type=f32)
    return jnp.dot(gelu(before).astype(bf16), down_rows, preferred_element_type=f32)


def mlp_sets(core_ref, sets, kept_refs, hidden_ref, acc_ref, given, up_buf, down_buf, sems, kept_sems):
    kept = []
    for index, pairs in enumerate(sets):
        slot = index % 2
        if index + 1 < len(sets):
            start_set(core_ref, sets[index + 1], up_buf, down_buf, sems, 1 - slot)
        wait_set(pairs, up_buf, down_buf, sems, slot)
        for kind, buf in enumerate((up_buf, down_buf)):
            place = 2 * index + kind
            kept.append(pltpu.make_async_copy(buf.at[slot], kept_refs[place], kept_sems.at[place]))
            kept[-1].start()
        part = mlp_part(hidden_ref[...], up_buf[slot], down_buf[slot])
        if index > 0:
            acc_ref[...] += part
        elif given is None:
            acc_ref[...] = part
        else:
            acc_ref[...] = given[...] + part
    for copy in kept:
        copy.wait()


def as_sets(refs):
    pairs = [(refs[i], refs[i + 1]) for i in range(0, len(refs), 2)]
    return [pairs[i : i + THIRDS] for i in range(0, len(pairs), THIRDS)]


def weight_scratch(units, width, slots):
    return [
        pltpu.VMEM((slots, units, width), bf16),
        pltpu.VMEM((slots, units, width), bf16),
        pltpu.SemaphoreType.DMA((slots, 2, THIRDS)),
        pltpu.SemaphoreType.DMA((2 * slots,)),
    ]


def kept_shapes(units, width, slots):
    return [jax.ShapeDtypeStruct((units, width), bf16)] * (2 * slots)


def flat_sets(sets):
    return [array for pairs in sets for pair in pairs for array in pair]


SMEM = pl.BlockSpec(memory_space=pltpu.SMEM)
VMEM = pl.BlockSpec(memory_space=pltpu.VMEM)
ANY = pl.BlockSpec(memory_space=pl.ANY)
HBM = pl.BlockSpec(memory_space=pltpu.HBM)
MIB = 2**20


def room(mebibytes):
    return pltpu.CompilerParams(vmem_limit_bytes=mebibytes * MIB)


def modulated(state, shift_row, scale_row):
    mean = jnp.mean(state, axis=1, keepdims=True)
    centred = state - mean
    var = jnp.mean(centred * centred, axis=1, keepdims=True)
    normed = centred * lax.rsqrt(var + EPSILON)
    return (normed * (1.0 + scale_row) + shift_row).astype(bf16)


def block_of(place, rows):
    return pl.ds(pl.multiple_of(place * rows, rows), rows)


def own_kernel(count, core_ref, state_ref, mod_ref, *refs):
    sets = as_sets(refs[:count])
    hidden_ref, acc_ref, *weights = refs[count:]
    kept, weights = weights[:2], weights[2:]
    start_set(core_ref, sets[0], *weights[:3], 0)
    tokens, width = state_ref.shape

    def one(place, carry):
        rows = block_of(place, ROWS)
        hidden_ref[rows, :] = modulated(
            state_ref[rows, :], mod_ref[OWN_ROW, 0:width], mod_ref[OWN_ROW, width : 2 * width]
        )
        return carry

    lax.fori_loop(0, tokens // ROWS, one, 0)
    mlp_sets(core_ref, sets, kept, hidden_ref, acc_ref, None, *weights)


def own_piece(core, state, mod, sets):
    weights = flat_sets(sets)
    units = THIRDS * weights[0].shape[0]
    tokens, width = state.shape
    return pl.pallas_call(
        functools.partial(own_kernel, len(weights)),
        out_shape=[jax.ShapeDtypeStruct((tokens, width), bf16), jax.ShapeDtypeStruct((tokens, width), f32)]
        + kept_shapes(units, width, 1),
        in_specs=[SMEM, VMEM, VMEM] + [ANY] * len(weights),
        out_specs=[VMEM, VMEM, HBM, HBM],
        scratch_shapes=weight_scratch(units, width, 1),
        compiler_params=room(56),
        name="own_piece",
    )(core, state, mod, *weights)


def fetch(pairs, sems):
    copies = [pltpu.make_async_copy(array, buf, sems.at[index]) for index, (array, buf) in enumerate(pairs)]
    for copy in copies:
        copy.start()
    return copies


def next_kernel(count, core_ref, hidden_in, acc_in, *refs):
    sets = as_sets(refs[:count])
    acc_ref, *weights = refs[count:]
    kept, (hidden_ref, given_ref, own_sems), weights = weights[:4], weights[4:7], weights[7:]
    start_set(core_ref, sets[0], *weights[:3], 0)
    for copy in fetch([(hidden_in, hidden_ref), (acc_in, given_ref)], own_sems):
        copy.wait()
    mlp_sets(core_ref, sets, kept, hidden_ref, acc_ref, given_ref, *weights)


def next_piece(core, hidden, acc, sets):
    weights = flat_sets(sets)
    units = THIRDS * weights[0].shape[0]
    tokens, width = hidden.shape
    return pl.pallas_call(
        functools.partial(next_kernel, len(weights)),
        out_shape=[jax.ShapeDtypeStruct((tokens, width), f32)] + kept_shapes(units, width, 2),
        in_specs=[SMEM, ANY, ANY] + [ANY] * len(weights),
        out_specs=[VMEM] + [HBM] * 4,
        scratch_shapes=[
            pltpu.VMEM((tokens, width), bf16),
            pltpu.VMEM((tokens, width), f32),
            pltpu.SemaphoreType.DMA((2,)),
        ]
        + weight_scratch(units, width, 2),
        compiler_params=room(56),
        name="next_piece",
    )(core, hidden, acc, *weights)


def far_kernel(
    count, core_ref, first_ref, begin_ref, dt_ref, sigma_ref, hidden_in, acc_in, state_ref, noise_ref, mod_ref, *refs
):
    sets = as_sets(refs[:count])
    out_ref, up_kept, down_kept, hidden_ref, given_ref, acc_ref, state_buf, noise_buf, own_sems, *weights = refs[count:]
    start_set(core_ref, sets[0], *weights[:3], 0)
    own = fetch(
        [(hidden_in, hidden_ref), (acc_in, given_ref), (state_ref, state_buf), (noise_ref, noise_buf)], own_sems
    )
    for copy in own[:2]:
        copy.wait()
    mlp_sets(core_ref, sets, [up_kept, down_kept], hidden_ref, acc_ref, given_ref, *weights)
    for copy in own[2:]:
        copy.wait()
    peers, rows, width = out_ref.shape
    rows = rows // 2
    step = begin_ref[0]

    def one(peer, carry):
        place = block_of(peer, rows)
        state = state_buf[place, :]
        drift = mod_ref[OWN_ROW, 2 * width : 3 * width] * acc_ref[place, :] - state
        inc = dt_ref[step] * drift + sigma_ref[step] * noise_buf[0, place, :].astype(f32)
        out_ref[peer, 0:rows, :] = (inc + first_ref[0] * state).astype(bf16)
        out_ref[peer, rows : 2 * rows, :] = noise_buf[1, place, :]
        return carry

    lax.fori_loop(0, peers, one, 0)


def far_piece(core, is_first, step, dt, sigma, hidden, acc, state, noise, mod, sets, peers):
    weights = flat_sets(sets)
    units = THIRDS * weights[0].shape[0]
    tokens, width = hidden.shape
    return pl.pallas_call(
        functools.partial(far_kernel, len(weights)),
        out_shape=[jax.ShapeDtypeStruct((peers, 2 * (tokens // peers), width), bf16)]
        + kept_shapes(units, width, 1),
        in_specs=[SMEM] * 5 + [ANY] * 4 + [VMEM] + [ANY] * len(weights),
        out_specs=[VMEM, HBM, HBM],
        scratch_shapes=[
            pltpu.VMEM((tokens, width), bf16),
            pltpu.VMEM((tokens, width), f32),
            pltpu.VMEM((tokens, width), f32),
            pltpu.VMEM(state.shape, f32),
            pltpu.VMEM(noise.shape, bf16),
            pltpu.SemaphoreType.DMA((4,)),
        ]
        + weight_scratch(units, width, 1),
        compiler_params=room(56),
        name="far_piece",
    )(core, is_first, step, dt, sigma, hidden, acc, state, noise, mod, *weights)


def second_kernel(count, begin_ref, advance_ref, dt_ref, sigma_ref, got_ref, mod_ref, *refs):
    sets = [(refs[i], refs[i + 1]) for i in range(0, count, 2)]
    out_ref, prefix_ref, hidden_ref, acc_ref, up_buf, down_buf, sems = refs[count:]

    def copies(index):
        slot = index % 2
        return [
            pltpu.make_async_copy(sets[index][kind], buf.at[slot], sems.at[slot, kind, 0])
            for kind, buf in enumerate((up_buf, down_buf))
        ]

    for copy in copies(0):
        copy.start()
    window, rows, width = out_ref.shape
    advance = advance_ref[0]
    begin = begin_ref[0] + advance

    total = got_ref[0, 0:rows, :].astype(f32)
    for place in range(1, window + SLIDE):
        prefix_ref[place] = total
        if place < window:
            total = total + got_ref[place, 0:rows, :].astype(f32)

    def modulate(place, carry):
        row = pl.ds(place, 1)
        hidden_ref[block_of(place, rows), :] = modulated(
            prefix_ref[place + advance], mod_ref[row, 0:width], mod_ref[row, width : 2 * width]
        )
        return carry

    lax.fori_loop(0, window, modulate, 0)
    for index in range(len(sets)):
        if index + 1 < len(sets):
            for copy in copies(index + 1):
                copy.start()
        for copy in copies(index):
            copy.wait()
        part = mlp_part(hidden_ref[...], up_buf[index % 2], down_buf[index % 2])
        acc_ref[...] = part if index == 0 else acc_ref[...] + part

    def update(place, updated):
        out_ref[place] = updated.astype(bf16)
        gate = mod_ref[pl.ds(place, 1), 2 * width : 3 * width]
        drift = gate * acc_ref[block_of(place, rows), :] - prefix_ref[place + advance]
        noise = got_ref[place, rows : 2 * rows, :].astype(f32)
        return updated + (dt_ref[begin + place] * drift + sigma_ref[begin + place] * noise)

    lax.fori_loop(0, window, update, prefix_ref[advance])


def second_sweep(begin, advance, dt, sigma, got, mod, weights):
    units = weights[0].shape[0]
    window, rows, width = got.shape
    rows = rows // 2
    return pl.pallas_call(
        functools.partial(second_kernel, len(weights)),
        out_shape=jax.ShapeDtypeStruct((window, rows, width), bf16),
        in_specs=[SMEM] * 4 + [VMEM] * 2 + [HBM] * len(weights),
        out_specs=VMEM,
        scratch_shapes=[
            pltpu.VMEM((window + SLIDE, rows, width), f32),
            pltpu.VMEM((window * rows, width), bf16),
            pltpu.VMEM((window * rows, width), f32),
        ]
        + weight_scratch(units, width, 2)[:3],
        compiler_params=room(56),
        name="second_sweep",
    )(begin, advance, dt, sigma, got, mod, *weights)


def time_embed(steps_now, half_width):
    frequency = jnp.exp(-math.log(10000.0) * jnp.arange(half_width, dtype=f32) / half_width)
    angles = steps_now.astype(f32)[:, None] * frequency[None, :]
    return jnp.concatenate([jnp.cos(angles), jnp.sin(angles)], axis=1)


def after(array, *others):
    return lax.optimization_barrier((array, *others))[0]


def per_device(
    state, noise_draws, class_vec, window_start, advance, step_dt, step_sigma, w_ada, w_up, w_down
):
    window = lax.axis_size("tm")
    core = lax.axis_index("batch") % CORES
    core_arg = core.astype(jnp.int32)[None]
    state, noise = state[0, 0], noise_draws[:, 0, 0]
    tokens, width = state.shape

    other = swap_cores(jnp.where(core == 0, w_down, w_up))
    rows = jnp.where(
        core == 0, jnp.concatenate([w_up, other]), jnp.concatenate([other, w_down])
    )
    third = rows.shape[0] // THIRDS
    parts = [rows[i * third : (i + 1) * third] for i in range(THIRDS)]
    orders = [(0, 1, 2), (1, 2, 0), (2, 0, 1)]
    for phase in range(2):
        parts = [grow(part, order[phase], core) for part, order in zip(parts, orders)]

    begin, ahead = window_start[0], advance[0]
    own_step = begin + lax.axis_index("tm")
    steps = begin + ahead + jnp.arange(window, dtype=jnp.int32)
    steps = jnp.concatenate([steps, jnp.full((8,), own_step, jnp.int32)])
    condition = jax.nn.silu(time_embed(steps, width // 2) + class_vec).astype(bf16)
    modulation = jnp.dot(condition, w_ada, preferred_element_type=f32)
    is_first = (lax.axis_index("tm") == 0).astype(f32)[None]

    last = [order[2] for order in orders]
    parts = [after(part, *parts) for part in parts]
    first = [send(part, axis, True) for part, axis in zip(parts, last)]
    ready = [after(part, near, modulation) for part, near in zip(parts, first)]
    second = [send(part, axis, False) for part, axis in zip(ready, last)]
    own_swapped = [swap_cores(after(part, modulation)) for part in parts]
    set_own = list(zip(parts, own_swapped))
    hidden, acc, *kept = own_piece(core_arg, state, modulation, [set_own])
    first_swapped = [swap_cores(after(part, acc)) for part in first]
    far = [send(after(near, other, acc), axis, False) for near, other, axis in zip(first, second, last)]
    second_swapped = [swap_cores(part) for part in second]
    set_low = list(zip(first, second_swapped))
    set_high = list(zip(second, first_swapped))
    acc, *more = next_piece(core_arg, hidden, acc, [set_low, set_high])
    kept += more

    far_swapped = [swap_cores(after(part, acc)) for part in far]
    set_far = list(zip(far, far_swapped))
    sent, *more = far_piece(
        core_arg, is_first, own_step[None], step_dt, step_sigma, hidden, acc, state, noise, modulation, [set_far], window
    )
    got = lax.all_to_all(sent, "tm", 0, 0, tiled=True)
    updated = second_sweep(
        window_start,
        advance,
        step_dt,
        step_sigma,
        got,
        modulation,
        kept + more,
    )
    final = lax.all_to_all(updated, "tm", 0, 0, tiled=True)
    return final.reshape(1, 1, tokens, width).astype(f32)


def solution(mesh):
    in_specs = (
        P("tm", "batch", None, None),
        P(None, "tm", "batch", None, None),
        P("batch", None),
        P("batch"),
        P("batch"),
        P(),
        P(),
        P(),
        P(("tm", "batch"), None),
        P(("tm", "batch"), None),
    )
    out_specs = P("tm", "batch", None, None)
    return jax.shard_map(
        per_device, mesh=mesh, in_specs=in_specs, out_specs=out_specs, check_vma=False
    )
```

```python
import functools
import math

import jax
import jax.numpy as jnp
from jax import lax
from jax.experimental import pallas as pl
from jax.experimental.pallas import tpu as pltpu
from jax.sharding import PartitionSpec as P

EPSILON = 1e-06
ALL = ("tm", "batch")
SIDE = 4
CORES = 2
THIRDS = 3
SLIDE = 7
ROWS = 16
OWN_ROW = slice(16, 17)
f32, bf16 = jnp.float32, jnp.bfloat16


def device_pairs(move):
    pairs = []
    for x in range(SIDE):
        for z in range(SIDE):
            for y in range(SIDE):
                for core in range(CORES):
                    here, there = (x, z, y, core), move((x, z, y, core))
                    flat = [((p[0] * SIDE + p[1]) * SIDE + p[2]) * CORES + p[3] for p in (here, there)]
                    pairs.append(tuple(flat))
    return pairs


def neighbour(axis, first):
    def move(place):
        place = list(place)
        odd = (place[3] == 0) == first
        place[axis] = place[axis] ^ 1 if odd else SIDE - 1 - place[axis]
        return tuple(place)

    return device_pairs(move)


def send(rows, axis, first):
    return lax.ppermute(rows, ALL, neighbour(axis, first))


def swap_cores(rows):
    return lax.ppermute(rows, ALL, device_pairs(lambda p: (p[0], p[1], p[2], 1 - p[3])))


def grow(rows, axis, core):
    near = send(rows, axis, True)
    both = send(jnp.concatenate([rows, near]), axis, False)
    count = rows.shape[0]
    second, far = both[:count], both[count:]
    low = jnp.where(core == 0, near, second)
    high = jnp.where(core == 0, second, near)
    return jnp.concatenate([rows, low, high, far])


def gelu(before):
    inner = math.sqrt(2.0 / math.pi) * (before + 0.044715 * (before * before * before))
    return 0.5 * before * (1.0 + jnp.tanh(inner))


def copies(side, pairs, up_buf, down_buf, sems, slot):
    made = []
    size = pairs[0][0].shape[0]
    for part, pair in enumerate(pairs):
        place = pl.ds(part * size, size)
        made.append(pltpu.make_async_copy(pair[side], up_buf.at[slot, place], sems.at[slot, 0, part]))
        made.append(
            pltpu.make_async_copy(pair[1 - side], down_buf.at[slot, place], sems.at[slot, 1, part])
        )
    return made


def start_set(core_ref, *where):
    for side in (0, 1):

        @pl.when(core_ref[0] == side)
        def _():
            for copy in copies(side, *where):
                copy.start()


def wait_set(*where):
    for copy in copies(0, *where):
        copy.wait()


def mlp_part(hidden, up_rows, down_rows):
    before = lax.dot_general(hidden, up_rows, (((1,), (1,)), ((), ())), preferred_element_type=f32)
    return jnp.dot(gelu(before).astype(bf16), down_rows, preferred_element_type=f32)


def mlp_sets(core_ref, sets, kept_refs, hidden_ref, acc_ref, given, up_buf, down_buf, sems, kept_sems):
    kept = []

    def keep(index):
        for kind, buf in enumerate((up_buf, down_buf)):
            place = 2 * index + kind
            kept.append(pltpu.make_async_copy(buf.at[index % 2], kept_refs[place], kept_sems.at[place]))
            kept[-1].start()

    for index, pairs in enumerate(sets):
        slot = index % 2
        if index + 1 < len(sets):
            start_set(core_ref, sets[index + 1], up_buf, down_buf, sems, 1 - slot)
        wait_set(pairs, up_buf, down_buf, sems, slot)
        if index + 1 == len(sets):
            for done in range(len(sets)):
                keep(done)
        part = mlp_part(hidden_ref[...], up_buf[slot], down_buf[slot])
        if index > 0:
            acc_ref[...] += part
        elif given is None:
            acc_ref[...] = part
        else:
            acc_ref[...] = given[...] + part
    for copy in kept:
        copy.wait()


def as_sets(refs):
    pairs = [(refs[i], refs[i + 1]) for i in range(0, len(refs), 2)]
    return [pairs[i : i + THIRDS] for i in range(0, len(pairs), THIRDS)]


def weight_scratch(units, width, slots):
    return [
        pltpu.VMEM((slots, units, width), bf16),
        pltpu.VMEM((slots, units, width), bf16),
        pltpu.SemaphoreType.DMA((slots, 2, THIRDS)),
        pltpu.SemaphoreType.DMA((2 * slots,)),
    ]


def kept_shapes(units, width, slots):
    return [jax.ShapeDtypeStruct((units, width), bf16)] * (2 * slots)


def flat_sets(sets):
    return [array for pairs in sets for pair in pairs for array in pair]


SMEM = pl.BlockSpec(memory_space=pltpu.SMEM)
VMEM = pl.BlockSpec(memory_space=pltpu.VMEM)
ANY = pl.BlockSpec(memory_space=pl.ANY)
HBM = pl.BlockSpec(memory_space=pltpu.HBM)
MIB = 2**20


def room(mebibytes):
    return pltpu.CompilerParams(vmem_limit_bytes=mebibytes * MIB)


def modulated(state, shift_row, scale_row):
    mean = jnp.mean(state, axis=1, keepdims=True)
    centred = state - mean
    var = jnp.mean(centred * centred, axis=1, keepdims=True)
    normed = centred * lax.rsqrt(var + EPSILON)
    return (normed * (1.0 + scale_row) + shift_row).astype(bf16)


def block_of(place, rows):
    return pl.ds(pl.multiple_of(place * rows, rows), rows)


def own_kernel(count, core_ref, state_ref, mod_ref, *refs):
    sets = as_sets(refs[:count])
    hidden_ref, acc_ref, *weights = refs[count:]
    kept, weights = weights[:2], weights[2:]
    start_set(core_ref, sets[0], *weights[:3], 0)
    tokens, width = state_ref.shape

    def one(place, carry):
        rows = block_of(place, ROWS)
        hidden_ref[rows, :] = modulated(
            state_ref[rows, :], mod_ref[OWN_ROW, 0:width], mod_ref[OWN_ROW, width : 2 * width]
        )
        return carry

    lax.fori_loop(0, tokens // ROWS, one, 0)
    mlp_sets(core_ref, sets, kept, hidden_ref, acc_ref, None, *weights)


def own_piece(core, state, mod, sets):
    weights = flat_sets(sets)
    units = THIRDS * weights[0].shape[0]
    tokens, width = state.shape
    return pl.pallas_call(
        functools.partial(own_kernel, len(weights)),
        out_shape=[jax.ShapeDtypeStruct((tokens, width), bf16), jax.ShapeDtypeStruct((tokens, width), f32)]
        + kept_shapes(units, width, 1),
        in_specs=[SMEM, VMEM, VMEM] + [ANY] * len(weights),
        out_specs=[VMEM, VMEM, HBM, HBM],
        scratch_shapes=weight_scratch(units, width, 1),
        compiler_params=room(56),
        name="own_piece",
    )(core, state, mod, *weights)


def fetch(pairs, sems):
    copies = [pltpu.make_async_copy(array, buf, sems.at[index]) for index, (array, buf) in enumerate(pairs)]
    for copy in copies:
        copy.start()
    return copies


def next_kernel(count, core_ref, hidden_in, acc_in, *refs):
    sets = as_sets(refs[:count])
    acc_ref, *weights = refs[count:]
    kept, (hidden_ref, given_ref, own_sems), weights = weights[:4], weights[4:7], weights[7:]
    start_set(core_ref, sets[0], *weights[:3], 0)
    for copy in fetch([(hidden_in, hidden_ref), (acc_in, given_ref)], own_sems):
        copy.wait()
    mlp_sets(core_ref, sets, kept, hidden_ref, acc_ref, given_ref, *weights)


def next_piece(core, hidden, acc, sets):
    weights = flat_sets(sets)
    units = THIRDS * weights[0].shape[0]
    tokens, width = hidden.shape
    return pl.pallas_call(
        functools.partial(next_kernel, len(weights)),
        out_shape=[jax.ShapeDtypeStruct((tokens, width), f32)] + kept_shapes(units, width, 2),
        in_specs=[SMEM, ANY, ANY] + [ANY] * len(weights),
        out_specs=[VMEM] + [HBM] * 4,
        scratch_shapes=[
            pltpu.VMEM((tokens, width), bf16),
            pltpu.VMEM((tokens, width), f32),
            pltpu.SemaphoreType.DMA((2,)),
        ]
        + weight_scratch(units, width, 2),
        compiler_params=room(56),
        name="next_piece",
    )(core, hidden, acc, *weights)


def far_kernel(
    count, core_ref, first_ref, begin_ref, dt_ref, sigma_ref, hidden_in, acc_in, state_ref, noise_ref, mod_ref, *refs
):
    sets = as_sets(refs[:count])
    out_ref, up_kept, down_kept, hidden_ref, given_ref, acc_ref, state_buf, noise_buf, own_sems, *weights = refs[count:]
    start_set(core_ref, sets[0], *weights[:3], 0)
    own = fetch(
        [(hidden_in, hidden_ref), (acc_in, given_ref), (state_ref, state_buf), (noise_ref, noise_buf)], own_sems
    )
    for copy in own[:2]:
        copy.wait()
    mlp_sets(core_ref, sets, [up_kept, down_kept], hidden_ref, acc_ref, given_ref, *weights)
    for copy in own[2:]:
        copy.wait()
    peers, rows, width = out_ref.shape
    rows = rows // 2
    step = begin_ref[0]

    def one(peer, carry):
        place = block_of(peer, rows)
        state = state_buf[place, :]
        drift = mod_ref[OWN_ROW, 2 * width : 3 * width] * acc_ref[place, :] - state
        inc = dt_ref[step] * drift + sigma_ref[step] * noise_buf[0, place, :].astype(f32)
        out_ref[peer, 0:rows, :] = (inc + first_ref[0] * state).astype(bf16)
        out_ref[peer, rows : 2 * rows, :] = noise_buf[1, place, :]
        return carry

    lax.fori_loop(0, peers, one, 0)


def far_piece(core, is_first, step, dt, sigma, hidden, acc, state, noise, mod, sets, peers):
    weights = flat_sets(sets)
    units = THIRDS * weights[0].shape[0]
    tokens, width = hidden.shape
    return pl.pallas_call(
        functools.partial(far_kernel, len(weights)),
        out_shape=[jax.ShapeDtypeStruct((peers, 2 * (tokens // peers), width), bf16)]
        + kept_shapes(units, width, 1),
        in_specs=[SMEM] * 5 + [ANY] * 4 + [VMEM] + [ANY] * len(weights),
        out_specs=[VMEM, HBM, HBM],
        scratch_shapes=[
            pltpu.VMEM((tokens, width), bf16),
            pltpu.VMEM((tokens, width), f32),
            pltpu.VMEM((tokens, width), f32),
            pltpu.VMEM(state.shape, f32),
            pltpu.VMEM(noise.shape, bf16),
            pltpu.SemaphoreType.DMA((4,)),
        ]
        + weight_scratch(units, width, 1),
        compiler_params=room(56),
        name="far_piece",
    )(core, is_first, step, dt, sigma, hidden, acc, state, noise, mod, *weights)


def second_kernel(count, begin_ref, advance_ref, dt_ref, sigma_ref, got_ref, mod_ref, *refs):
    sets = [(refs[i], refs[i + 1]) for i in range(0, count, 2)]
    out_ref, prefix_ref, hidden_ref, acc_ref, up_buf, down_buf, sems = refs[count:]

    def copies(index):
        slot = index % 2
        return [
            pltpu.make_async_copy(sets[index][kind], buf.at[slot], sems.at[slot, kind, 0])
            for kind, buf in enumerate((up_buf, down_buf))
        ]

    for copy in copies(0):
        copy.start()
    window, rows, width = out_ref.shape
    advance = advance_ref[0]
    begin = begin_ref[0] + advance

    total = got_ref[0, 0:rows, :].astype(f32)
    for place in range(1, window + SLIDE):
        prefix_ref[place] = total
        if place < window:
            total = total + got_ref[place, 0:rows, :].astype(f32)

    def modulate(place, carry):
        row = pl.ds(place, 1)
        hidden_ref[block_of(place, rows), :] = modulated(
            prefix_ref[place + advance], mod_ref[row, 0:width], mod_ref[row, width : 2 * width]
        )
        return carry

    lax.fori_loop(0, window - 1, modulate, 0)
    for index in range(len(sets)):
        if index + 1 < len(sets):
            for copy in copies(index + 1):
                copy.start()
        for copy in copies(index):
            copy.wait()
        part = mlp_part(hidden_ref[...], up_buf[index % 2], down_buf[index % 2])
        acc_ref[...] = part if index == 0 else acc_ref[...] + part

    def update(place, updated):
        out_ref[place] = updated.astype(bf16)
        gate = mod_ref[pl.ds(place, 1), 2 * width : 3 * width]
        drift = gate * acc_ref[block_of(place, rows), :] - prefix_ref[place + advance]
        noise = got_ref[place, rows : 2 * rows, :].astype(f32)
        return updated + (dt_ref[begin + place] * drift + sigma_ref[begin + place] * noise)

    out_ref[window - 1] = lax.fori_loop(0, window - 1, update, prefix_ref[advance]).astype(bf16)


def second_sweep(begin, advance, dt, sigma, got, mod, weights):
    units = weights[0].shape[0]
    window, rows, width = got.shape
    rows = rows // 2
    return pl.pallas_call(
        functools.partial(second_kernel, len(weights)),
        out_shape=jax.ShapeDtypeStruct((window, rows, width), bf16),
        in_specs=[SMEM] * 4 + [VMEM] * 2 + [HBM] * len(weights),
        out_specs=VMEM,
        scratch_shapes=[
            pltpu.VMEM((window + SLIDE, rows, width), f32),
            pltpu.VMEM(((window - 1) * rows, width), bf16),
            pltpu.VMEM(((window - 1) * rows, width), f32),
        ]
        + weight_scratch(units, width, 2)[:3],
        compiler_params=room(56),
        name="second_sweep",
    )(begin, advance, dt, sigma, got, mod, *weights)


def time_embed(steps_now, half_width):
    frequency = jnp.exp(-math.log(10000.0) * jnp.arange(half_width, dtype=f32) / half_width)
    angles = steps_now.astype(f32)[:, None] * frequency[None, :]
    return jnp.concatenate([jnp.cos(angles), jnp.sin(angles)], axis=1)


def after(array, *others):
    return lax.optimization_barrier((array, *others))[0]


def per_device(
    state, noise_draws, class_vec, window_start, advance, step_dt, step_sigma, w_ada, w_up, w_down
):
    window = lax.axis_size("tm")
    core = lax.axis_index("batch") % CORES
    core_arg = core.astype(jnp.int32)[None]
    state, noise = state[0, 0], noise_draws[:, 0, 0]
    tokens, width = state.shape

    other = swap_cores(jnp.where(core == 0, w_down, w_up))
    rows = jnp.where(
        core == 0, jnp.concatenate([w_up, other]), jnp.concatenate([other, w_down])
    )
    third = rows.shape[0] // THIRDS
    parts = [rows[i * third : (i + 1) * third] for i in range(THIRDS)]
    orders = [(0, 1, 2), (1, 2, 0), (2, 0, 1)]
    for phase in range(2):
        parts = [grow(part, order[phase], core) for part, order in zip(parts, orders)]

    begin, ahead = window_start[0], advance[0]
    own_step = begin + lax.axis_index("tm")
    steps = begin + ahead + jnp.arange(window, dtype=jnp.int32)
    steps = jnp.concatenate([steps, jnp.full((8,), own_step, jnp.int32)])
    condition = jax.nn.silu(time_embed(steps, width // 2) + class_vec).astype(bf16)
    modulation = jnp.dot(condition, w_ada, preferred_element_type=f32)
    is_first = (lax.axis_index("tm") == 0).astype(f32)[None]

    last = [order[2] for order in orders]
    parts = [after(part, *parts) for part in parts]
    first = [send(part, axis, True) for part, axis in zip(parts, last)]
    ready = [after(part, near, modulation) for part, near in zip(parts, first)]
    second = [send(part, axis, False) for part, axis in zip(ready, last)]
    own_swapped = [swap_cores(after(part, modulation)) for part in parts]
    set_own = list(zip(parts, own_swapped))
    hidden, acc, *kept = own_piece(core_arg, state, modulation, [set_own])
    first_swapped = [swap_cores(after(part, acc)) for part in first]
    far = [send(after(near, other, acc), axis, False) for near, other, axis in zip(first, second, last)]
    second_swapped = [swap_cores(part) for part in second]
    set_low = list(zip(first, second_swapped))
    set_high = list(zip(second, first_swapped))
    acc, *more = next_piece(core_arg, hidden, acc, [set_low, set_high])
    kept += more

    far_swapped = [swap_cores(after(part, acc)) for part in far]
    set_far = list(zip(far, far_swapped))
    sent, *more = far_piece(
        core_arg, is_first, own_step[None], step_dt, step_sigma, hidden, acc, state, noise, modulation, [set_far], window
    )
    got = lax.all_to_all(sent, "tm", 0, 0, tiled=True)
    updated = second_sweep(
        window_start,
        advance,
        step_dt,
        step_sigma,
        got,
        modulation,
        kept + more,
    )
    final = lax.all_to_all(updated, "tm", 0, 0, tiled=True)
    return final.reshape(1, 1, tokens, width).astype(f32)


def solution(mesh):
    in_specs = (
        P("tm", "batch", None, None),
        P(None, "tm", "batch", None, None),
        P("batch", None),
        P("batch"),
        P("batch"),
        P(),
        P(),
        P(),
        P(("tm", "batch"), None),
        P(("tm", "batch"), None),
    )
    out_specs = P("tm", "batch", None, None)
    return jax.shard_map(
        per_device, mesh=mesh, in_specs=in_specs, out_specs=out_specs, check_vma=False
    )
```

```python
import functools
import math

import jax
import jax.numpy as jnp
from jax import lax
from jax.experimental import pallas as pl
from jax.experimental.pallas import tpu as pltpu
from jax.sharding import PartitionSpec as P

EPSILON = 1e-06
ALL = ("tm", "batch")
SIDE = 4
CORES = 2
THIRDS = 3
SLIDE = 7
ROWS = 16
OWN_ROW = slice(16, 17)
f32, bf16 = jnp.float32, jnp.bfloat16


def device_pairs(move):
    pairs = []
    for x in range(SIDE):
        for z in range(SIDE):
            for y in range(SIDE):
                for core in range(CORES):
                    here, there = (x, z, y, core), move((x, z, y, core))
                    flat = [((p[0] * SIDE + p[1]) * SIDE + p[2]) * CORES + p[3] for p in (here, there)]
                    pairs.append(tuple(flat))
    return pairs


def neighbour(axis, first):
    def move(place):
        place = list(place)
        odd = (place[3] == 0) == first
        place[axis] = place[axis] ^ 1 if odd else SIDE - 1 - place[axis]
        return tuple(place)

    return device_pairs(move)


def send(rows, axis, first):
    return lax.ppermute(rows, ALL, neighbour(axis, first))


def swap_cores(rows):
    return lax.ppermute(rows, ALL, device_pairs(lambda p: (p[0], p[1], p[2], 1 - p[3])))


def grow(rows, axis, core):
    near = send(rows, axis, True)
    both = send(jnp.concatenate([rows, near]), axis, False)
    count = rows.shape[0]
    second, far = both[:count], both[count:]
    low = jnp.where(core == 0, near, second)
    high = jnp.where(core == 0, second, near)
    return jnp.concatenate([rows, low, high, far])


def gelu(before):
    inner = math.sqrt(2.0 / math.pi) * (before + 0.044715 * (before * before * before))
    return 0.5 * before * (1.0 + jnp.tanh(inner))


def copies(side, pairs, up_buf, down_buf, sems, slot):
    made = []
    size = pairs[0][0].shape[0]
    for part, pair in enumerate(pairs):
        place = pl.ds(part * size, size)
        made.append(pltpu.make_async_copy(pair[side], up_buf.at[slot, place], sems.at[slot, 0, part]))
        made.append(
            pltpu.make_async_copy(pair[1 - side], down_buf.at[slot, place], sems.at[slot, 1, part])
        )
    return made


def start_set(core_ref, *where):
    for side in (0, 1):

        @pl.when(core_ref[0] == side)
        def _():
            for copy in copies(side, *where):
                copy.start()


def wait_set(*where):
    for copy in copies(0, *where):
        copy.wait()


def mlp_part(hidden, up_rows, down_rows):
    before = lax.dot_general(hidden, up_rows, (((1,), (1,)), ((), ())), preferred_element_type=f32)
    return jnp.dot(gelu(before).astype(bf16), down_rows, preferred_element_type=f32)


def mlp_sets(core_ref, sets, kept_refs, hidden_ref, acc_ref, given, up_buf, down_buf, sems, kept_sems):
    kept = []

    def keep(index):
        for kind, buf in enumerate((up_buf, down_buf)):
            place = 2 * index + kind
            kept.append(pltpu.make_async_copy(buf.at[index % 2], kept_refs[place], kept_sems.at[place]))
            kept[-1].start()

    for index, pairs in enumerate(sets):
        slot = index % 2
        if index + 1 < len(sets):
            start_set(core_ref, sets[index + 1], up_buf, down_buf, sems, 1 - slot)
        wait_set(pairs, up_buf, down_buf, sems, slot)
        if index + 1 == len(sets):
            for done in range(len(sets)):
                keep(done)
        part = mlp_part(hidden_ref[...], up_buf[slot], down_buf[slot])
        if index > 0:
            acc_ref[...] += part
        elif given is None:
            acc_ref[...] = part
        else:
            acc_ref[...] = given[...] + part
    for copy in kept:
        copy.wait()


def as_sets(refs):
    pairs = [(refs[i], refs[i + 1]) for i in range(0, len(refs), 2)]
    return [pairs[i : i + THIRDS] for i in range(0, len(pairs), THIRDS)]


def weight_scratch(units, width, slots):
    return [
        pltpu.VMEM((slots, units, width), bf16),
        pltpu.VMEM((slots, units, width), bf16),
        pltpu.SemaphoreType.DMA((slots, 2, THIRDS)),
        pltpu.SemaphoreType.DMA((2 * slots,)),
    ]


def kept_shapes(units, width, slots):
    return [jax.ShapeDtypeStruct((units, width), bf16)] * (2 * slots)


def flat_sets(sets):
    return [array for pairs in sets for pair in pairs for array in pair]


SMEM = pl.BlockSpec(memory_space=pltpu.SMEM)
VMEM = pl.BlockSpec(memory_space=pltpu.VMEM)
ANY = pl.BlockSpec(memory_space=pl.ANY)
HBM = pl.BlockSpec(memory_space=pltpu.HBM)
MIB = 2**20


def room(mebibytes):
    return pltpu.CompilerParams(vmem_limit_bytes=mebibytes * MIB)


def modulated(state, shift_row, scale_row):
    mean = jnp.mean(state, axis=1, keepdims=True)
    centred = state - mean
    var = jnp.mean(centred * centred, axis=1, keepdims=True)
    normed = centred * lax.rsqrt(var + EPSILON)
    return (normed * (1.0 + scale_row) + shift_row).astype(bf16)


def block_of(place, rows):
    return pl.ds(pl.multiple_of(place * rows, rows), rows)


def own_kernel(count, core_ref, state_in, mod_in, *refs):
    sets = as_sets(refs[:count])
    hidden_ref, acc_ref, *weights = refs[count:]
    kept, (state_ref, mod_ref, own_sems), weights = weights[:2], weights[2:5], weights[5:]
    own = fetch([(state_in, state_ref), (mod_in, mod_ref)], own_sems)
    start_set(core_ref, sets[0], *weights[:3], 0)
    for copy in own:
        copy.wait()
    tokens, width = state_ref.shape

    def one(place, carry):
        rows = block_of(place, ROWS)
        hidden_ref[rows, :] = modulated(
            state_ref[rows, :], mod_ref[OWN_ROW, 0:width], mod_ref[OWN_ROW, width : 2 * width]
        )
        return carry

    lax.fori_loop(0, tokens // ROWS, one, 0)
    mlp_sets(core_ref, sets, kept, hidden_ref, acc_ref, None, *weights)


def own_piece(core, state, mod, sets):
    weights = flat_sets(sets)
    units = THIRDS * weights[0].shape[0]
    tokens, width = state.shape
    return pl.pallas_call(
        functools.partial(own_kernel, len(weights)),
        out_shape=[jax.ShapeDtypeStruct((tokens, width), bf16), jax.ShapeDtypeStruct((tokens, width), f32)]
        + kept_shapes(units, width, 1),
        in_specs=[SMEM, ANY, ANY] + [ANY] * len(weights),
        out_specs=[VMEM, VMEM, HBM, HBM],
        scratch_shapes=[
            pltpu.VMEM(state.shape, f32),
            pltpu.VMEM(mod.shape, f32),
            pltpu.SemaphoreType.DMA((2,)),
        ]
        + weight_scratch(units, width, 1),
        compiler_params=room(56),
        name="own_piece",
    )(core, state, mod, *weights)


def fetch(pairs, sems):
    copies = [pltpu.make_async_copy(array, buf, sems.at[index]) for index, (array, buf) in enumerate(pairs)]
    for copy in copies:
        copy.start()
    return copies


def next_kernel(count, core_ref, hidden_in, acc_in, *refs):
    sets = as_sets(refs[:count])
    acc_ref, *weights = refs[count:]
    kept, (hidden_ref, given_ref, own_sems), weights = weights[:4], weights[4:7], weights[7:]
    start_set(core_ref, sets[0], *weights[:3], 0)
    for copy in fetch([(hidden_in, hidden_ref), (acc_in, given_ref)], own_sems):
        copy.wait()
    mlp_sets(core_ref, sets, kept, hidden_ref, acc_ref, given_ref, *weights)


def next_piece(core, hidden, acc, sets):
    weights = flat_sets(sets)
    units = THIRDS * weights[0].shape[0]
    tokens, width = hidden.shape
    return pl.pallas_call(
        functools.partial(next_kernel, len(weights)),
        out_shape=[jax.ShapeDtypeStruct((tokens, width), f32)] + kept_shapes(units, width, 2),
        in_specs=[SMEM, ANY, ANY] + [ANY] * len(weights),
        out_specs=[VMEM] + [HBM] * 4,
        scratch_shapes=[
            pltpu.VMEM((tokens, width), bf16),
            pltpu.VMEM((tokens, width), f32),
            pltpu.SemaphoreType.DMA((2,)),
        ]
        + weight_scratch(units, width, 2),
        compiler_params=room(56),
        name="next_piece",
    )(core, hidden, acc, *weights)


def far_kernel(
    count, core_ref, first_ref, begin_ref, dt_ref, sigma_ref, hidden_in, acc_in, state_ref, noise_ref, mod_ref, *refs
):
    sets = as_sets(refs[:count])
    out_ref, up_kept, down_kept, hidden_ref, given_ref, acc_ref, state_buf, noise_buf, own_sems, *weights = refs[count:]
    start_set(core_ref, sets[0], *weights[:3], 0)
    own = fetch(
        [(hidden_in, hidden_ref), (acc_in, given_ref), (state_ref, state_buf), (noise_ref, noise_buf)], own_sems
    )
    for copy in own[:2]:
        copy.wait()
    mlp_sets(core_ref, sets, [up_kept, down_kept], hidden_ref, acc_ref, given_ref, *weights)
    for copy in own[2:]:
        copy.wait()
    peers, rows, width = out_ref.shape
    rows = rows // 2
    step = begin_ref[0]

    def one(peer, carry):
        place = block_of(peer, rows)
        state = state_buf[place, :]
        drift = mod_ref[OWN_ROW, 2 * width : 3 * width] * acc_ref[place, :] - state
        inc = dt_ref[step] * drift + sigma_ref[step] * noise_buf[0, place, :].astype(f32)
        out_ref[peer, 0:rows, :] = (inc + first_ref[0] * state).astype(bf16)
        out_ref[peer, rows : 2 * rows, :] = noise_buf[1, place, :]
        return carry

    lax.fori_loop(0, peers, one, 0)


def far_piece(core, is_first, step, dt, sigma, hidden, acc, state, noise, mod, sets, peers):
    weights = flat_sets(sets)
    units = THIRDS * weights[0].shape[0]
    tokens, width = hidden.shape
    return pl.pallas_call(
        functools.partial(far_kernel, len(weights)),
        out_shape=[jax.ShapeDtypeStruct((peers, 2 * (tokens // peers), width), bf16)]
        + kept_shapes(units, width, 1),
        in_specs=[SMEM] * 5 + [ANY] * 4 + [VMEM] + [ANY] * len(weights),
        out_specs=[VMEM, HBM, HBM],
        scratch_shapes=[
            pltpu.VMEM((tokens, width), bf16),
            pltpu.VMEM((tokens, width), f32),
            pltpu.VMEM((tokens, width), f32),
            pltpu.VMEM(state.shape, f32),
            pltpu.VMEM(noise.shape, bf16),
            pltpu.SemaphoreType.DMA((4,)),
        ]
        + weight_scratch(units, width, 1),
        compiler_params=room(56),
        name="far_piece",
    )(core, is_first, step, dt, sigma, hidden, acc, state, noise, mod, *weights)


def second_kernel(count, begin_ref, advance_ref, dt_ref, sigma_ref, got_ref, mod_ref, *refs):
    sets = [(refs[i], refs[i + 1]) for i in range(0, count, 2)]
    out_ref, prefix_ref, hidden_ref, acc_ref, up_buf, down_buf, sems = refs[count:]

    def copies(index):
        slot = index % 2
        return [
            pltpu.make_async_copy(sets[index][kind], buf.at[slot], sems.at[slot, kind, 0])
            for kind, buf in enumerate((up_buf, down_buf))
        ]

    for copy in copies(0):
        copy.start()
    window, rows, width = out_ref.shape
    advance = advance_ref[0]
    begin = begin_ref[0] + advance

    total = got_ref[0, 0:rows, :].astype(f32)
    for place in range(1, window + SLIDE):
        prefix_ref[place] = total
        if place < window:
            total = total + got_ref[place, 0:rows, :].astype(f32)

    def modulate(place, carry):
        row = pl.ds(place, 1)
        hidden_ref[block_of(place, rows), :] = modulated(
            prefix_ref[place + advance], mod_ref[row, 0:width], mod_ref[row, width : 2 * width]
        )
        return carry

    lax.fori_loop(0, window - 1, modulate, 0)
    for index in range(len(sets)):
        if index + 1 < len(sets):
            for copy in copies(index + 1):
                copy.start()
        for copy in copies(index):
            copy.wait()
        part = mlp_part(hidden_ref[...], up_buf[index % 2], down_buf[index % 2])
        acc_ref[...] = part if index == 0 else acc_ref[...] + part

    def update(place, updated):
        out_ref[place] = updated.astype(bf16)
        gate = mod_ref[pl.ds(place, 1), 2 * width : 3 * width]
        drift = gate * acc_ref[block_of(place, rows), :] - prefix_ref[place + advance]
        noise = got_ref[place, rows : 2 * rows, :].astype(f32)
        return updated + (dt_ref[begin + place] * drift + sigma_ref[begin + place] * noise)

    out_ref[window - 1] = lax.fori_loop(0, window - 1, update, prefix_ref[advance]).astype(bf16)


def second_sweep(begin, advance, dt, sigma, got, mod, weights):
    units = weights[0].shape[0]
    window, rows, width = got.shape
    rows = rows // 2
    return pl.pallas_call(
        functools.partial(second_kernel, len(weights)),
        out_shape=jax.ShapeDtypeStruct((window, rows, width), bf16),
        in_specs=[SMEM] * 4 + [VMEM] * 2 + [HBM] * len(weights),
        out_specs=VMEM,
        scratch_shapes=[
            pltpu.VMEM((window + SLIDE, rows, width), f32),
            pltpu.VMEM(((window - 1) * rows, width), bf16),
            pltpu.VMEM(((window - 1) * rows, width), f32),
        ]
        + weight_scratch(units, width, 2)[:3],
        compiler_params=room(56),
        name="second_sweep",
    )(begin, advance, dt, sigma, got, mod, *weights)


def time_embed(steps_now, half_width):
    frequency = jnp.exp(-math.log(10000.0) * jnp.arange(half_width, dtype=f32) / half_width)
    angles = steps_now.astype(f32)[:, None] * frequency[None, :]
    return jnp.concatenate([jnp.cos(angles), jnp.sin(angles)], axis=1)


def after(array, *others):
    return lax.optimization_barrier((array, *others))[0]


def per_device(
    state, noise_draws, class_vec, window_start, advance, step_dt, step_sigma, w_ada, w_up, w_down
):
    window = lax.axis_size("tm")
    core = lax.axis_index("batch") % CORES
    core_arg = core.astype(jnp.int32)[None]
    state, noise = state[0, 0], noise_draws[:, 0, 0]
    tokens, width = state.shape

    other = swap_cores(jnp.where(core == 0, w_down, w_up))
    rows = jnp.where(
        core == 0, jnp.concatenate([w_up, other]), jnp.concatenate([other, w_down])
    )
    third = rows.shape[0] // THIRDS
    parts = [rows[i * third : (i + 1) * third] for i in range(THIRDS)]
    orders = [(0, 1, 2), (1, 2, 0), (2, 0, 1)]
    for phase in range(2):
        parts = [grow(part, order[phase], core) for part, order in zip(parts, orders)]

    begin, ahead = window_start[0], advance[0]
    own_step = begin + lax.axis_index("tm")
    steps = begin + ahead + jnp.arange(window, dtype=jnp.int32)
    steps = jnp.concatenate([steps, jnp.full((8,), own_step, jnp.int32)])
    condition = jax.nn.silu(time_embed(steps, width // 2) + class_vec).astype(bf16)
    modulation = jnp.dot(condition, w_ada, preferred_element_type=f32)
    is_first = (lax.axis_index("tm") == 0).astype(f32)[None]

    last = [order[2] for order in orders]
    parts = [after(part, *parts) for part in parts]
    first = [send(part, axis, True) for part, axis in zip(parts, last)]
    ready = [after(part, near, modulation) for part, near in zip(parts, first)]
    second = [send(part, axis, False) for part, axis in zip(ready, last)]
    own_swapped = [swap_cores(after(part, modulation)) for part in parts]
    set_own = list(zip(parts, own_swapped))
    hidden, acc, *kept = own_piece(core_arg, state, modulation, [set_own])
    first_swapped = [swap_cores(after(part, acc)) for part in first]
    far = [send(after(near, other, acc), axis, False) for near, other, axis in zip(first, second, last)]
    second_swapped = [swap_cores(part) for part in second]
    set_low = list(zip(first, second_swapped))
    set_high = list(zip(second, first_swapped))
    acc, *more = next_piece(core_arg, hidden, acc, [set_low, set_high])
    kept += more

    far_swapped = [swap_cores(after(part, acc)) for part in far]
    set_far = list(zip(far, far_swapped))
    sent, *more = far_piece(
        core_arg, is_first, own_step[None], step_dt, step_sigma, hidden, acc, state, noise, modulation, [set_far], window
    )
    got = lax.all_to_all(sent, "tm", 0, 0, tiled=True)
    updated = second_sweep(
        window_start,
        advance,
        step_dt,
        step_sigma,
        got,
        modulation,
        kept + more,
    )
    final = lax.all_to_all(updated, "tm", 0, 0, tiled=True)
    return final.reshape(1, 1, tokens, width).astype(f32)


def solution(mesh):
    in_specs = (
        P("tm", "batch", None, None),
        P(None, "tm", "batch", None, None),
        P("batch", None),
        P("batch"),
        P("batch"),
        P(),
        P(),
        P(),
        P(("tm", "batch"), None),
        P(("tm", "batch"), None),
    )
    out_specs = P("tm", "batch", None, None)
    return jax.shard_map(
        per_device, mesh=mesh, in_specs=in_specs, out_specs=out_specs, check_vma=False
    )
```
